32 devices in a mesh: groups: 2 (over x), hid: 8 (over z, y), ffn: 2 (over core).
Axes of the slice: x: 2, y: 2, z: 4, core: 2. Of those that a mesh axis runs over, the one named last changes fastest.
Arguments:
- hidden_in: bfloat16 [192, 16384], P('groups', 'hid'), parts along dimension 0, may hold values from -6 to 6
- w_query: bfloat16 [16384, 8192], P('hid', 'ffn'), may hold values from -0.046875 to 0.046875
- w_key: bfloat16 [16384, 512], P('hid', 'ffn'), may hold values from -0.046875 to 0.046875
- w_value: bfloat16 [16384, 512], P('hid', 'ffn'), may hold values from -0.046875 to 0.046875
- w_out: bfloat16 [8192, 16384], P('ffn', 'hid'), may hold values from -0.25 to 0.25
- key_cache: bfloat16 [192, 256, 4, 128], P(('groups', 'hid'), None, 'ffn'), parts along dimension 0
- value_cache: bfloat16 [192, 256, 4, 128], P(('groups', 'hid'), None, 'ffn'), parts along dimension 0, may hold values from -6 to 6
- lengths: int32 [192], P(('groups', 'hid')), parts along dimension 0, may hold values from 1 to 256, as said below
- slot_pos: int32 [192, 256], P(('groups', 'hid')), parts along dimension 0, may hold values from 0 to 255, each once within a row
Outputs:
- block_out: bfloat16 [192, 16384], P(('groups', 'ffn'), 'hid'), parts along dimension 0
The draws below stay inside these ranges and needn't reach their ends.
There are 2 independent parts, one for each index of `groups`. The reference program is written for one: setup_inputs(seed, part) draws one part's arguments, and reference() takes and returns one part's arrays. A program takes and returns all parts, laid end to end along the dimension named above; an argument that names none is the same for every part. Nothing has to cross between parts.
Inputs may be any that keep to these rules, and one draw needn't show every extreme that they name: `slot_pos`: each row of a request's slots holds every position 0 to 255 exactly once. `lengths`: some request has exactly 256 earlier tokens.
All inputs are finite; a program needn't handle non-finite values.
Results may differ from the reference program's by a relative error of at most 0.012.
Values may be sent and summed in bfloat16 or wider, within the bound.
A program may use at most 128 MiB of HBM per device.

```python
import jax
import jax.numpy as jnp
from jax import lax

D = 16384
HQ = 64
KVH = 4
HD = 128
CTX = 256
ROWS = 96


def draw_key_cache(key, part):
    key = jax.random.fold_in(key, 11)
    shape = (ROWS, CTX, KVH, HD)
    return jax.random.normal(key, shape, jnp.float32).astype(jnp.bfloat16)


def draw_lengths(key, part):
    key = jax.random.fold_in(key, 5)
    first, second, third = jax.random.split(key, 3)
    upper = jax.random.randint(first, (ROWS,), 1, CTX + 1)
    counts = jax.random.randint(second, (ROWS,), 1, upper + 1)
    where_full = jax.random.randint(third, (), 0, ROWS)
    return counts.at[where_full].set(CTX).astype(jnp.int32)


def block_levels(stream_key, dims, pieces, low, high):
    def one(dim, blocks):
        steps = jax.random.uniform(jax.random.fold_in(jax.random.fold_in(stream_key, 6), dim), (blocks,), jnp.float32, low / len(pieces), high / len(pieces))
        return jnp.repeat(jnp.exp(steps), dims[dim] // blocks).reshape((-1,) + (1,) * (len(dims) - dim - 1))

    gain = one(*pieces[0])
    for cut in pieces[1:]:
        gain = gain * one(*cut)
    return gain


def scatter_about(rng, dims, scale, bound, cuts=(), held_as=jnp.bfloat16):
    entries = jax.random.normal(rng, dims, jnp.float32) * scale
    if len(cuts) > 0:
        entries = block_levels(rng, dims, cuts, -0.22, 0.18) * entries
    return jnp.clip(entries, min=-bound, max=bound).astype(held_as)


def setup_inputs(seed: int = 0, part: int = 0) -> dict:
    seeds = jax.random.split(jax.random.key(seed), 10)
    own_keys = jax.random.split(jax.random.fold_in(seeds[9], part), 10)
    hidden_in = scatter_about(own_keys[0], (ROWS, D), 1.0, 6.0, ((1, 8),))
    w_query = scatter_about(seeds[1], (D, HQ * HD), D ** -0.5, 0.046875, ((0, 8), (1, 2)))
    w_key = scatter_about(seeds[2], (D, KVH * HD), D ** -0.5, 0.046875, ((0, 8), (1, 2)))
    w_value = scatter_about(seeds[3], (D, KVH * HD), D ** -0.5, 0.046875, ((0, 8), (1, 2)))
    w_out = scatter_about(seeds[4], (HQ * HD, D), (HQ * HD // 16) ** -0.5, 0.25, ((0, 2), (1, 8)))
    key_cache = draw_key_cache(jax.random.fold_in(jax.random.fold_in(seeds[9], part), 71), part)
    value_cache = scatter_about(own_keys[6], (ROWS, CTX, KVH, HD), 1.0, 6.0, ((0, 8), (2, 2)))
    lengths = draw_lengths(jax.random.fold_in(jax.random.fold_in(seeds[9], part), 71), part)
    slot_pos = jax.vmap(lambda own: jax.random.permutation(own, CTX))(jax.random.split(own_keys[8], ROWS)).reshape((ROWS, CTX)).astype(jnp.int32)
    return dict(hidden_in=hidden_in, w_query=w_query, w_key=w_key, w_value=w_value, w_out=w_out, key_cache=key_cache, value_cache=value_cache, lengths=lengths, slot_pos=slot_pos)


def rotate(tensor, pos):
    half = tensor.shape[-1] // 2
    freq = 500000.0 ** (-(jnp.arange(half, dtype=jnp.float32) * 2.0) / tensor.shape[-1])
    angle = pos[:, None, None] * freq[None, None, :]
    cosine = jnp.cos(angle)
    sine = jnp.sin(angle)
    first = tensor[..., :half]
    second = tensor[..., half:]
    return jnp.concatenate([first * cosine - second * sine, second * cosine + first * sine], axis=-1)

def reference(hidden_in, w_query, w_key, w_value, w_out, key_cache, value_cache, lengths, slot_pos):
    group = HQ // KVH
    query = jnp.dot(hidden_in, w_query, preferred_element_type=jnp.float32).reshape(ROWS, HQ, HD)
    new_key = jnp.dot(hidden_in, w_key, preferred_element_type=jnp.float32).reshape(ROWS, KVH, HD)
    new_value = jnp.dot(hidden_in, w_value, preferred_element_type=jnp.float32).reshape(ROWS, KVH, HD)
    pos = lengths.astype(jnp.float32)
    rot_query = rotate(query, pos).astype(jnp.bfloat16)
    rot_key = rotate(new_key, pos).astype(jnp.bfloat16)
    value_b = new_value.astype(jnp.bfloat16)
    scale = 1.0 / jnp.sqrt(jnp.float32(HD))
    grouped = rot_query.reshape(ROWS, KVH, group, HD).astype(jnp.float32)
    scores = jnp.einsum('rgjd,rtgd->rgjt', grouped, key_cache.astype(jnp.float32)) * scale
    live = slot_pos < lengths[:, None]
    scores = jnp.where(live[:, None, None, :], scores, -jnp.inf)
    own = jnp.einsum('rgjd,rgd->rgj', grouped, rot_key.astype(jnp.float32)) * scale
    top = jnp.maximum(lax.optimization_barrier(jnp.max(scores, axis=-1)), own)
    expo = jnp.exp(scores - top[..., None])
    own_expo = jnp.exp(own - top)
    total = lax.optimization_barrier(jnp.sum(expo, axis=-1)) + own_expo
    weights = (expo / total[..., None]).astype(jnp.bfloat16)
    own_weight = (own_expo / total).astype(jnp.bfloat16)
    attended = jnp.einsum('rgjt,rtgd->rgjd', weights.astype(jnp.float32), value_cache.astype(jnp.float32))
    attended = attended + own_weight.astype(jnp.float32)[..., None] * value_b.astype(jnp.float32)[:, :, None, :]
    attended = attended.reshape(ROWS, HQ * HD).astype(jnp.bfloat16)
    return jnp.dot(attended, w_out, preferred_element_type=jnp.float32).astype(jnp.bfloat16)
```

```python
import functools
import math

import jax
import jax.numpy as jnp
from jax import lax
from jax.experimental import pallas as pl
from jax.experimental.pallas import tpu as pltpu
from jax.sharding import PartitionSpec as P

HD = 128
NH = 8
MESH = pl.DeviceIdType.MESH
F32 = jnp.float32
BF16 = jnp.bfloat16


def kernel(
    nb,
    len_ref, slot_ref, x_hbm, wq_hbm, wk_hbm, wv_hbm, wo_hbm, kc_hbm, vc_hbm,
    out_ref,
    x, wq, wkv, wo, kc, vc,
    fkv, fq, skv, sq, rkv, rq,
    cos_s, sin_s, qf, kvf, sc, of, ag, lf, lhs, acc, fin,
    local_sem, rs_send, rs_recv, ag_send, ag_recv, fin_send, fin_recv,
):
    hid = 1 << nb
    h = lax.axis_index("hid")
    f = lax.axis_index("ffn")
    my = [lax.rem(lax.div(h, 1 << b), 2) for b in range(nb)]
    partner = [h + (1 - 2 * my[b]) * (1 << b) for b in range(nb)]
    rows = x.shape[0]
    rb = rows // hid
    nq = wq.shape[0]
    qw = wq.shape[2]
    order = tuple(range(nb))

    cp_x = pltpu.make_async_copy(x_hbm, x, local_sem.at[0])
    cp_k = pltpu.make_async_copy(wk_hbm, wkv.at[0], local_sem.at[1])
    cp_v = pltpu.make_async_copy(wv_hbm, wkv.at[1], local_sem.at[2])
    cp_kc = pltpu.make_async_copy(kc_hbm, kc, local_sem.at[3])
    cp_vc = pltpu.make_async_copy(vc_hbm, vc, local_sem.at[4])
    cp_q = [
        pltpu.make_async_copy(wq_hbm.at[:, pl.ds(c * qw, qw)], wq.at[c], local_sem.at[5 + c])
        for c in range(nq)
    ]
    cp_o = [
        pltpu.make_async_copy(
            wo_hbm.at[pl.ds(c * qw, qw), :], wo.at[c], local_sem.at[5 + nq + c]
        )
        for c in range(nq)
    ]
    cp_x.start()
    cp_k.start()
    cp_v.start()
    cp_q[0].start()
    cp_q[1].start()

    barrier = pltpu.get_barrier_semaphore()
    for b in range(nb):
        pl.semaphore_signal(barrier, inc=1, device_id={"hid": partner[b]}, device_id_type=MESH)
    pl.semaphore_signal(barrier, inc=1, device_id={"ffn": 1 - f}, device_id_type=MESH)

    lane = lax.broadcasted_iota(jnp.int32, (1, HD), 1)
    idx = jnp.where(lane < HD // 2, lane, lane - HD // 2).astype(F32)
    freq = jnp.exp(idx * (-2.0 * math.log(500000.0) / HD))
    for r in range(rb):
        cos_s[r : r + 1, :] = len_ref[r].astype(F32) * freq
    angle = cos_s[...]
    sign = jnp.where(lane < HD // 2, -1.0, 1.0).astype(F32)
    sin_s[...] = jnp.sin(angle) * sign
    cos_s[...] = jnp.cos(angle)

    def bufs(c):
        if c == 0:
            return fkv, skv, rkv, rb * 4
        return fq.at[c - 1], sq.at[c - 1], rq.at[c - 1], rb * NH

    def rs_copy(c, k):
        _, s, r, block = bufs(c)
        count = hid >> (k + 1)
        start = hid - (hid >> k)
        part = pl.ds(start * block, count * block)
        return pltpu.make_async_remote_copy(
            src_ref=s.at[part], dst_ref=r.at[part],
            send_sem=rs_send.at[c * nb + k], recv_sem=rs_recv.at[c * nb + k],
            device_id={"hid": partner[order[k]]}, device_id_type=MESH,
        )

    def rs_stage(c, k):
        sums, s, r, block = bufs(c)
        if k > 0:
            rs_copy(c, k - 1).wait_recv()
        left = nb - k - 1
        start = hid - (hid >> k)
        before = hid - (hid >> (k - 1)) if k > 0 else 0
        base = 0
        for j in range(k):
            base = base + my[order[j]] * (1 << order[j])

        def at(i, bit):
            off = 0
            for m in range(left):
                off += ((i >> (left - 1 - m)) & 1) << order[k + 1 + m]
            t = base + bit * (1 << order[k]) + off
            return pl.ds(pl.multiple_of(t * block, block), block)

        def came(i, bit):
            p = before + bit * (1 << left) + i
            return pl.ds(pl.multiple_of(p * block, block), block)

        mine = my[order[k]]
        for i in range(1 << left):
            value = sums[at(i, 1 - mine), :]
            if k > 0:
                value = value + r[came(i, 1 - mine), :].astype(F32)
            s[pl.ds((start + i) * block, block), :] = value.astype(BF16)
        rs_copy(c, k).start()
        if k > 0:
            for i in range(1 << left):
                sums[at(i, mine), :] = sums[at(i, mine), :] + r[came(i, mine), :].astype(F32)

    def rs_final(c):
        sums, s, r, block = bufs(c)
        rs_copy(c, nb - 1).wait_recv()
        own = pl.ds(pl.multiple_of(h * block, block), block)
        value = sums[own, :] + r[pl.ds((hid - 2) * block, block), :].astype(F32)
        if c == 0:
            kvf[...] = value
            return
        value = value.reshape(rb, NH, HD)
        turned = pltpu.roll(value.reshape(rb * NH, HD), HD // 2, 1).reshape(rb, NH, HD)
        cosine = cos_s[...][:, None, :]
        sine = sin_s[...][:, None, :]
        qf[:, (c - 1) * NH : c * NH, :] = value * cosine + turned * sine

    cp_x.wait()
    for part, cp in ((0, cp_k), (1, cp_v)):
        cp.wait()
        got = jnp.dot(x[...], wkv[part], preferred_element_type=F32)
        for j in range(2):
            fkv[pl.ds(part * 2 + j, rows, stride=4), :] = got[:, j * HD : (j + 1) * HD]
    pl.semaphore_wait(barrier, nb + 1)
    rs_stage(0, 0)

    wave = []
    for c in range(nq):
        cp_q[c].wait()
        if c + 2 < nq:
            cp_q[c + 2].start()
        elif c + 2 == nq:
            cp_kc.start()
            cp_vc.start()
            cp_o[0].start()
        else:
            for o in range(1, nq):
                cp_o[o].start()

        @pl.loop(0, qw // 256)
        def _(n):
            cols = pl.ds(pl.multiple_of(n * 256, 256), 256)
            got = jnp.dot(x[...], wq.at[c][:, cols], preferred_element_type=F32)
            for j in range(2):
                fq.at[c][pl.ds(n * 2 + j, rows, stride=NH), :] = got[:, j * HD : (j + 1) * HD]

        rs_stage(c + 1, 0)
        if c > 0:
            rs_stage(c - 1, 1)

    done = {(c, 0) for c in range(nq + 1)} | {(c, 1) for c in range(nq - 1)}
    for w in range(nq + 1 + nb):
        for k in range(nb, 0, -1):
            c = w - k
            if 0 <= c <= nq and (c, k) not in done:
                if k == nb:
                    rs_final(c)
                else:
                    rs_stage(c, k)

    heads = nq * NH
    slots = slot_ref.shape[1]
    spread = (
        lax.broadcasted_iota(jnp.int32, (slots, 2 * slots), 0)
        == lax.div(lax.broadcasted_iota(jnp.int32, (slots, 2 * slots), 1), 2)
    )
    spread = jnp.where(spread, 1.0, 0.0).astype(BF16)
    position = jnp.dot(
        slot_ref[...].astype(F32).astype(BF16), spread, preferred_element_type=F32
    )
    parity = (
        lax.rem(lax.broadcasted_iota(jnp.int32, (heads, 2 * slots), 1), 2)
        == lax.div(lax.broadcasted_iota(jnp.int32, (heads, 2 * slots), 0), heads // 2)
    )
    scale = 1.0 / math.sqrt(HD)
    cp_kc.wait()
    cp_vc.wait()
    for r in range(rb):
        sc[r] = lax.dot_general(
            qf[r].astype(BF16), kc[r], (((1,), (1,)), ((), ())), preferred_element_type=F32
        )
    kvrot = kvf[...]
    turned = pltpu.roll(kvrot, HD // 2, 1)
    for r in range(rb):
        def both(first, second):
            return jnp.concatenate(
                [
                    jnp.broadcast_to(first, (heads // 2, HD)),
                    jnp.broadcast_to(second, (heads // 2, HD)),
                ],
                axis=0,
            )

        cosine = cos_s[r : r + 1, :]
        sine = sin_s[r : r + 1, :]
        key = [
            (kvrot[r * 4 + g : r * 4 + g + 1] * cosine + turned[r * 4 + g : r * 4 + g + 1] * sine)
            for g in range(2)
        ]
        key = both(*key).astype(BF16).astype(F32)
        value = both(kvrot[r * 4 + 2 : r * 4 + 3], kvrot[r * 4 + 3 : r * 4 + 4])
        value = value.astype(BF16).astype(F32)
        query = qf[r].astype(BF16).astype(F32)
        own = jnp.sum(query * key, axis=-1, keepdims=True) * scale
        live = position[r : r + 1, :] < len_ref[r].astype(F32)
        scores = jnp.where(live & parity, sc[r] * scale, -jnp.inf)
        top = jnp.maximum(jnp.max(scores, axis=-1, keepdims=True), own)
        expo = jnp.exp(scores - top)
        own_expo = jnp.exp(own - top)
        over = 1.0 / (jnp.sum(expo, axis=-1, keepdims=True) + own_expo)
        weights = (expo * over).astype(BF16)
        own_weight = (own_expo * over).astype(BF16).astype(F32)
        got = jnp.dot(weights, vc[r], preferred_element_type=F32) + own_weight * value
        for c in range(nq):
            of[c, r * NH : (r + 1) * NH, :] = got[c * NH : (c + 1) * NH]

    block = rb * NH
    place = 0
    for k in range(nb):
        place = place * 2 + my[order[k]]

    def ag_copy(c, k):
        start = lax.div(place, 1 << k) * (1 << k)
        part = pl.ds(pl.multiple_of(start * block, block), (1 << k) * block)
        return pltpu.make_async_remote_copy(
            src_ref=ag.at[c, part], dst_ref=ag.at[c, part],
            send_sem=ag_send.at[c * nb + k], recv_sem=ag_recv.at[c * nb + k],
            device_id={"hid": partner[order[nb - 1 - k]]}, device_id_type=MESH,
        )

    def position_of(t):
        p = 0
        for k in range(nb):
            p = p * 2 + ((t >> order[k]) & 1)
        return p

    half = rows // 2
    cols_out = out_ref.shape[1]
    tile = 512 if cols_out % 512 == 0 else cols_out
    tiles = cols_out // tile

    def fin_copy(n):
        cols = pl.ds(n * tile, tile)
        return pltpu.make_async_remote_copy(
            src_ref=acc.at[pl.ds(pl.multiple_of((1 - f) * half, half), half), cols],
            dst_ref=fin.at[:, cols],
            send_sem=fin_send.at[n], recv_sem=fin_recv.at[n],
            device_id={"ffn": 1 - f}, device_id_type=MESH,
        )

    def project(c):
        for t in range(hid):
            lf[t * block : (t + 1) * block, :] = ag[
                c, position_of(t) * block : (position_of(t) + 1) * block, :
            ].astype(F32)
        for j in range(NH):
            lhs[:, j * HD : (j + 1) * HD] = lf[pl.ds(j, rows, stride=NH), :].astype(BF16)
        cp_o[c].wait()
        for n in range(tiles):
            cols = pl.ds(n * tile, tile)
            got = jnp.dot(lhs[...], wo.at[c][:, cols], preferred_element_type=F32)
            if c == 0:
                acc[:, cols] = got
            else:
                acc[:, cols] = acc[:, cols] + got
            if c == nq - 1:
                fin_copy(n).start()

    for c in range(nq):
        own = pl.ds(pl.multiple_of(place * block, block), block)
        ag[c, own, :] = of[c].astype(BF16)
        ag_copy(c, 0).start()
    for w in range(1, nq + nb):
        for k in range(nb, 0, -1):
            c = w - k
            if 0 <= c < nq:
                ag_copy(c, k - 1).wait_recv()
                if k < nb:
                    ag_copy(c, k).start()
        c = w - nb
        if 0 <= c < nq:
            project(c)

    kept = pl.ds(pl.multiple_of(f * half, half), half)
    for n in range(tiles):
        cols = pl.ds(n * tile, tile)
        fin_copy(n).wait_recv()
        out_ref[:, cols] = (acc[kept, cols] + fin[:, cols]).astype(BF16)

    for c in range(nq + 1):
        for k in range(nb):
            rs_copy(c, k).wait_send()
    for c in range(nq):
        for k in range(nb):
            ag_copy(c, k).wait_send()
    for n in range(tiles):
        fin_copy(n).wait_send()


def per_device(hid, x, w_query, w_key, w_value, w_out, key_cache, value_cache, lengths, slot_pos):
    nb = hid.bit_length() - 1
    rows, depth = x.shape
    rb, slots, kvh, _ = key_cache.shape
    qcols = w_query.shape[1]
    qw = NH * HD
    nq = qcols // qw
    ncols = w_out.shape[1]
    tiles = ncols // 512 if ncols % 512 == 0 else 1
    kc = key_cache.reshape(rb, slots * kvh, HD)
    vc = value_cache.reshape(rb, slots * kvh, HD)
    anywhere = pl.BlockSpec(memory_space=pl.ANY)
    vmem = pltpu.VMEM
    return pl.pallas_call(
        functools.partial(kernel, nb),
        out_shape=jax.ShapeDtypeStruct((rows // 2, ncols), BF16),
        in_specs=[
            pl.BlockSpec(memory_space=pltpu.SMEM),
            pl.BlockSpec(memory_space=pltpu.VMEM),
        ] + [anywhere] * 7,
        out_specs=pl.BlockSpec(memory_space=pltpu.VMEM),
        scratch_shapes=[
            vmem((rows, depth), BF16),
            vmem((nq, depth, qw), BF16),
            vmem((2, depth, 2 * HD), BF16),
            vmem((nq, qw, ncols), BF16),
            vmem((rb, slots * kvh, HD), BF16),
            vmem((rb, slots * kvh, HD), BF16),
            vmem((rows * 4, HD), F32),
            vmem((nq, rows * NH, HD), F32),
            vmem(((hid - 1) * rb * 4, HD), BF16),
            vmem((nq, (hid - 1) * rb * NH, HD), BF16),
            vmem(((hid - 1) * rb * 4, HD), BF16),
            vmem((nq, (hid - 1) * rb * NH, HD), BF16),
            vmem((rb, HD), F32),
            vmem((rb, HD), F32),
            vmem((rb, nq * NH, HD), F32),
            vmem((rb * 4, HD), F32),
            vmem((rb, nq * NH, slots * kvh), F32),
            vmem((nq, rb * NH, HD), F32),
            vmem((nq, rows * NH, HD), BF16),
            vmem((rows * NH, HD), F32),
            vmem((rows, qw), BF16),
            vmem((rows, ncols), F32),
            vmem((rows // 2, ncols), F32),
            pltpu.SemaphoreType.DMA((5 + 2 * nq,)),
            pltpu.SemaphoreType.DMA(((nq + 1) * nb,)),
            pltpu.SemaphoreType.DMA(((nq + 1) * nb,)),
            pltpu.SemaphoreType.DMA((nq * nb,)),
            pltpu.SemaphoreType.DMA((nq * nb,)),
            pltpu.SemaphoreType.DMA((tiles,)),
            pltpu.SemaphoreType.DMA((tiles,)),
        ],
        compiler_params=pltpu.CompilerParams(
            collective_id=0, has_side_effects=True, vmem_limit_bytes=56 * 1024 * 1024
        ),
    )(lengths, slot_pos, x, w_query, w_key, w_value, w_out, kc, vc)


def solution(mesh):
    placed = (
        P("groups", "hid"),
        P("hid", "ffn"),
        P("hid", "ffn"),
        P("hid", "ffn"),
        P("ffn", "hid"),
        P(("groups", "hid"), None, "ffn", None),
        P(("groups", "hid"), None, "ffn", None),
        P(("groups", "hid")),
        P(("groups", "hid"), None),
    )
    return jax.shard_map(
        functools.partial(per_device, mesh.shape["hid"]),
        mesh=mesh,
        in_specs=placed,
        out_specs=P(("groups", "ffn"), "hid"),
        check_vma=False,
    )
```

```python
import functools
import math

import jax
import jax.numpy as jnp
from jax import lax
from jax.experimental import pallas as pl
from jax.experimental.pallas import tpu as pltpu
from jax.sharding import PartitionSpec as P

HD = 128
NH = 8
MESH = pl.DeviceIdType.MESH
F32 = jnp.float32
BF16 = jnp.bfloat16


def kernel(
    nb,
    len_ref, slot_ref, x_hbm, wq_hbm, wk_hbm, wv_hbm, wo_hbm, kc_hbm, vc_hbm,
    out_ref,
    x, wq, wkv, wo, kc, vc,
    fkv, fq, skv, sq, rkv, rq,
    cos_s, sin_s, qf, kvf, sc, of, ag, lf, lhs, acc, fin,
    local_sem, rs_send, rs_recv, ag_send, ag_recv, fin_send, fin_recv,
):
    hid = 1 << nb
    h = lax.axis_index("hid")
    f = lax.axis_index("ffn")
    my = [lax.rem(lax.div(h, 1 << b), 2) for b in range(nb)]
    partner = [h + (1 - 2 * my[b]) * (1 << b) for b in range(nb)]
    rows = x.shape[0]
    rb = rows // hid
    nq = wq.shape[0]
    qw = wq.shape[2]
    orders = [tuple(range(nb)), (1, 0) + tuple(range(2, nb)) if nb > 1 else (0,)]

    def order_of(c):
        return orders[(c + 1) % 2]

    cp_x = pltpu.make_async_copy(x_hbm, x, local_sem.at[0])
    cp_k = pltpu.make_async_copy(wk_hbm, wkv.at[0], local_sem.at[1])
    cp_v = pltpu.make_async_copy(wv_hbm, wkv.at[1], local_sem.at[2])
    cp_kc = pltpu.make_async_copy(kc_hbm, kc, local_sem.at[3])
    cp_vc = pltpu.make_async_copy(vc_hbm, vc, local_sem.at[4])
    cp_q = [
        pltpu.make_async_copy(wq_hbm.at[:, pl.ds(c * qw, qw)], wq.at[c], local_sem.at[5 + c])
        for c in range(nq)
    ]
    cp_o = [
        pltpu.make_async_copy(
            wo_hbm.at[pl.ds(c * qw, qw), :], wo.at[c], local_sem.at[5 + nq + c]
        )
        for c in range(nq)
    ]
    cp_x.start()
    cp_k.start()
    cp_v.start()
    cp_q[0].start()
    cp_q[1].start()

    barrier = pltpu.get_barrier_semaphore()
    for b in range(nb):
        pl.semaphore_signal(barrier, inc=1, device_id={"hid": partner[b]}, device_id_type=MESH)
    pl.semaphore_signal(barrier, inc=1, device_id={"ffn": 1 - f}, device_id_type=MESH)

    lane = lax.broadcasted_iota(jnp.int32, (1, HD), 1)
    idx = jnp.where(lane < HD // 2, lane, lane - HD // 2).astype(F32)
    freq = jnp.exp(idx * (-2.0 * math.log(500000.0) / HD))
    for r in range(rb):
        cos_s[r : r + 1, :] = len_ref[r].astype(F32) * freq
    angle = cos_s[...]
    sign = jnp.where(lane < HD // 2, -1.0, 1.0).astype(F32)
    sin_s[...] = jnp.sin(angle) * sign
    cos_s[...] = jnp.cos(angle)

    def bufs(c):
        if c == 0:
            return fkv, skv, rkv, rb * 4
        return fq.at[c - 1], sq.at[c - 1], rq.at[c - 1], rb * NH

    def rs_copy(c, k):
        order = order_of(c)
        _, s, r, block = bufs(c)
        count = hid >> (k + 1)
        start = hid - (hid >> k)
        part = pl.ds(start * block, count * block)
        return pltpu.make_async_remote_copy(
            src_ref=s.at[part], dst_ref=r.at[part],
            send_sem=rs_send.at[c * nb + k], recv_sem=rs_recv.at[c * nb + k],
            device_id={"hid": partner[order[k]]}, device_id_type=MESH,
        )

    def rs_stage(c, k):
        order = order_of(c)
        sums, s, r, block = bufs(c)
        if k > 0:
            rs_copy(c, k - 1).wait_recv()
        left = nb - k - 1
        start = hid - (hid >> k)
        before = hid - (hid >> (k - 1)) if k > 0 else 0
        base = 0
        for j in range(k):
            base = base + my[order[j]] * (1 << order[j])

        def at(i, bit):
            off = 0
            for m in range(left):
                off += ((i >> (left - 1 - m)) & 1) << order[k + 1 + m]
            t = base + bit * (1 << order[k]) + off
            return pl.ds(pl.multiple_of(t * block, block), block)

        def came(i, bit):
            p = before + bit * (1 << left) + i
            return pl.ds(pl.multiple_of(p * block, block), block)

        mine = my[order[k]]
        for i in range(1 << left):
            value = sums[at(i, 1 - mine), :]
            if k > 0:
                value = value + r[came(i, 1 - mine), :].astype(F32)
            s[pl.ds((start + i) * block, block), :] = value.astype(BF16)
        rs_copy(c, k).start()
        if k > 0:
            for i in range(1 << left):
                sums[at(i, mine), :] = sums[at(i, mine), :] + r[came(i, mine), :].astype(F32)

    def rs_final(c):
        sums, s, r, block = bufs(c)
        rs_copy(c, nb - 1).wait_recv()
        own = pl.ds(pl.multiple_of(h * block, block), block)
        value = sums[own, :] + r[pl.ds((hid - 2) * block, block), :].astype(F32)
        if c == 0:
            kvf[...] = value
            return
        value = value.reshape(rb, NH, HD)
        turned = pltpu.roll(value.reshape(rb * NH, HD), HD // 2, 1).reshape(rb, NH, HD)
        cosine = cos_s[...][:, None, :]
        sine = sin_s[...][:, None, :]
        qf[:, (c - 1) * NH : c * NH, :] = value * cosine + turned * sine

    cp_x.wait()
    for part, cp in ((0, cp_k), (1, cp_v)):
        cp.wait()
        got = jnp.dot(x[...], wkv[part], preferred_element_type=F32)
        for j in range(2):
            fkv[pl.ds(part * 2 + j, rows, stride=4), :] = got[:, j * HD : (j + 1) * HD]
    pl.semaphore_wait(barrier, nb + 1)
    rs_stage(0, 0)

    for c in range(nq):
        cp_q[c].wait()
        if c + 2 < nq:
            cp_q[c + 2].start()
        elif c + 2 == nq:
            cp_kc.start()
            cp_vc.start()
            cp_o[0].start()
        else:
            for o in range(1, nq):
                cp_o[o].start()

        @pl.loop(0, qw // 256)
        def _(n):
            cols = pl.ds(pl.multiple_of(n * 256, 256), 256)
            got = jnp.dot(x[...], wq.at[c][:, cols], preferred_element_type=F32)
            for j in range(2):
                fq.at[c][pl.ds(n * 2 + j, rows, stride=NH), :] = got[:, j * HD : (j + 1) * HD]

        rs_stage(c + 1, 0)
        for k in range(1, min(nb, c + 1)):
            rs_stage(c - k, k)

    done = {(c - k, k) for c in range(nq) for k in range(1, min(nb, c + 1))}
    for w in range(nq + 1 + nb):
        for k in range(nb, 0, -1):
            c = w - k
            if 0 <= c <= nq and (c, k) not in done:
                if k == nb:
                    rs_final(c)
                else:
                    rs_stage(c, k)

    heads = nq * NH
    slots = slot_ref.shape[1]
    spread = (
        lax.broadcasted_iota(jnp.int32, (slots, 2 * slots), 0)
        == lax.div(lax.broadcasted_iota(jnp.int32, (slots, 2 * slots), 1), 2)
    )
    spread = jnp.where(spread, 1.0, 0.0).astype(BF16)
    position = jnp.dot(
        slot_ref[...].astype(F32).astype(BF16), spread, preferred_element_type=F32
    )
    parity = (
        lax.rem(lax.broadcasted_iota(jnp.int32, (heads, 2 * slots), 1), 2)
        == lax.div(lax.broadcasted_iota(jnp.int32, (heads, 2 * slots), 0), heads // 2)
    )
    scale = 1.0 / math.sqrt(HD)
    cp_kc.wait()
    cp_vc.wait()
    for r in range(rb):
        sc[r] = lax.dot_general(
            qf[r].astype(BF16), kc[r], (((1,), (1,)), ((), ())), preferred_element_type=F32
        )
    kvrot = kvf[...]
    turned = pltpu.roll(kvrot, HD // 2, 1)
    for r in range(rb):
        def both(first, second):
            return jnp.concatenate(
                [
                    jnp.broadcast_to(first, (heads // 2, HD)),
                    jnp.broadcast_to(second, (heads // 2, HD)),
                ],
                axis=0,
            )

        cosine = cos_s[r : r + 1, :]
        sine = sin_s[r : r + 1, :]
        key = [
            (kvrot[r * 4 + g : r * 4 + g + 1] * cosine + turned[r * 4 + g : r * 4 + g + 1] * sine)
            for g in range(2)
        ]
        key = both(*key).astype(BF16).astype(F32)
        value = both(kvrot[r * 4 + 2 : r * 4 + 3], kvrot[r * 4 + 3 : r * 4 + 4])
        value = value.astype(BF16).astype(F32)
        query = qf[r].astype(BF16).astype(F32)
        own = jnp.sum(query * key, axis=-1, keepdims=True) * scale
        live = position[r : r + 1, :] < len_ref[r].astype(F32)
        scores = jnp.where(live & parity, sc[r] * scale, -jnp.inf)
        top = jnp.maximum(jnp.max(scores, axis=-1, keepdims=True), own)
        expo = jnp.exp(scores - top)
        own_expo = jnp.exp(own - top)
        over = 1.0 / (jnp.sum(expo, axis=-1, keepdims=True) + own_expo)
        weights = (expo * over).astype(BF16)
        own_weight = (own_expo * over).astype(BF16).astype(F32)
        got = jnp.dot(weights, vc[r], preferred_element_type=F32) + own_weight * value
        for c in range(nq):
            of[c, r * NH : (r + 1) * NH, :] = got[c * NH : (c + 1) * NH]

    block = rb * NH

    def place_of(c):
        place = 0
        for k in range(nb):
            place = place * 2 + my[order_of(c + 1)[k]]
        return place

    def ag_copy(c, k):
        start = lax.div(place_of(c), 1 << k) * (1 << k)
        part = pl.ds(pl.multiple_of(start * block, block), (1 << k) * block)
        return pltpu.make_async_remote_copy(
            src_ref=ag.at[c, part], dst_ref=ag.at[c, part],
            send_sem=ag_send.at[c * nb + k], recv_sem=ag_recv.at[c * nb + k],
            device_id={"hid": partner[order_of(c + 1)[nb - 1 - k]]}, device_id_type=MESH,
        )

    def position_of(c, t):
        p = 0
        for k in range(nb):
            p = p * 2 + ((t >> order_of(c + 1)[k]) & 1)
        return p

    half = rows // 2
    cols_out = out_ref.shape[1]
    tile = 512 if cols_out % 512 == 0 else cols_out
    tiles = cols_out // tile

    def fin_copy(n):
        cols = pl.ds(n * tile, tile)
        return pltpu.make_async_remote_copy(
            src_ref=acc.at[pl.ds(pl.multiple_of((1 - f) * half, half), half), cols],
            dst_ref=fin.at[:, cols],
            send_sem=fin_send.at[n], recv_sem=fin_recv.at[n],
            device_id={"ffn": 1 - f}, device_id_type=MESH,
        )

    def project(c):
        for t in range(hid):
            lf[t * block : (t + 1) * block, :] = ag[
                c, position_of(c, t) * block : (position_of(c, t) + 1) * block, :
            ].astype(F32)
        for j in range(NH):
            lhs[:, j * HD : (j + 1) * HD] = lf[pl.ds(j, rows, stride=NH), :].astype(BF16)
        cp_o[c].wait()
        for n in range(tiles):
            cols = pl.ds(n * tile, tile)
            got = jnp.dot(lhs[...], wo.at[c][:, cols], preferred_element_type=F32)
            if c == 0:
                acc[:, cols] = got
            else:
                acc[:, cols] = acc[:, cols] + got
            if c == nq - 1:
                fin_copy(n).start()

    for c in range(nq):
        own = pl.ds(pl.multiple_of(place_of(c) * block, block), block)
        ag[c, own, :] = of[c].astype(BF16)
        ag_copy(c, 0).start()
    for w in range(1, nq + nb):
        for k in range(nb, 0, -1):
            c = w - k
            if 0 <= c < nq:
                ag_copy(c, k - 1).wait_recv()
                if k < nb:
                    ag_copy(c, k).start()
        c = w - nb
        if 0 <= c < nq:
            project(c)

    kept = pl.ds(pl.multiple_of(f * half, half), half)
    for n in range(tiles):
        cols = pl.ds(n * tile, tile)
        fin_copy(n).wait_recv()
        out_ref[:, cols] = (acc[kept, cols] + fin[:, cols]).astype(BF16)

    for c in range(nq + 1):
        for k in range(nb):
            rs_copy(c, k).wait_send()
    for c in range(nq):
        for k in range(nb):
            ag_copy(c, k).wait_send()
    for n in range(tiles):
        fin_copy(n).wait_send()


def per_device(hid, x, w_query, w_key, w_value, w_out, key_cache, value_cache, lengths, slot_pos):
    nb = hid.bit_length() - 1
    rows, depth = x.shape
    rb, slots, kvh, _ = key_cache.shape
    qcols = w_query.shape[1]
    qw = NH * HD
    nq = qcols // qw
    ncols = w_out.shape[1]
    tiles = ncols // 512 if ncols % 512 == 0 else 1
    kc = key_cache.reshape(rb, slots * kvh, HD)
    vc = value_cache.reshape(rb, slots * kvh, HD)
    anywhere = pl.BlockSpec(memory_space=pl.ANY)
    vmem = pltpu.VMEM
    return pl.pallas_call(
        functools.partial(kernel, nb),
        out_shape=jax.ShapeDtypeStruct((rows // 2, ncols), BF16),
        in_specs=[
            pl.BlockSpec(memory_space=pltpu.SMEM),
            pl.BlockSpec(memory_space=pltpu.VMEM),
        ] + [anywhere] * 7,
        out_specs=pl.BlockSpec(memory_space=pltpu.VMEM),
        scratch_shapes=[
            vmem((rows, depth), BF16),
            vmem((nq, depth, qw), BF16),
            vmem((2, depth, 2 * HD), BF16),
            vmem((nq, qw, ncols), BF16),
            vmem((rb, slots * kvh, HD), BF16),
            vmem((rb, slots * kvh, HD), BF16),
            vmem((rows * 4, HD), F32),
            vmem((nq, rows * NH, HD), F32),
            vmem(((hid - 1) * rb * 4, HD), BF16),
            vmem((nq, (hid - 1) * rb * NH, HD), BF16),
            vmem(((hid - 1) * rb * 4, HD), BF16),
            vmem((nq, (hid - 1) * rb * NH, HD), BF16),
            vmem((rb, HD), F32),
            vmem((rb, HD), F32),
            vmem((rb, nq * NH, HD), F32),
            vmem((rb * 4, HD), F32),
            vmem((rb, nq * NH, slots * kvh), F32),
            vmem((nq, rb * NH, HD), F32),
            vmem((nq, rows * NH, HD), BF16),
            vmem((rows * NH, HD), F32),
            vmem((rows, qw), BF16),
            vmem((rows, ncols), F32),
            vmem((rows // 2, ncols), F32),
            pltpu.SemaphoreType.DMA((5 + 2 * nq,)),
            pltpu.SemaphoreType.DMA(((nq + 1) * nb,)),
            pltpu.SemaphoreType.DMA(((nq + 1) * nb,)),
            pltpu.SemaphoreType.DMA((nq * nb,)),
            pltpu.SemaphoreType.DMA((nq * nb,)),
            pltpu.SemaphoreType.DMA((tiles,)),
            pltpu.SemaphoreType.DMA((tiles,)),
        ],
        compiler_params=pltpu.CompilerParams(
            collective_id=0, has_side_effects=True, vmem_limit_bytes=56 * 1024 * 1024
        ),
    )(lengths, slot_pos, x, w_query, w_key, w_value, w_out, kc, vc)


def solution(mesh):
    placed = (
        P("groups", "hid"),
        P("hid", "ffn"),
        P("hid", "ffn"),
        P("hid", "ffn"),
        P("ffn", "hid"),
        P(("groups", "hid"), None, "ffn", None),
        P(("groups", "hid"), None, "ffn", None),
        P(("groups", "hid")),
        P(("groups", "hid"), None),
    )
    return jax.shard_map(
        functools.partial(per_device, mesh.shape["hid"]),
        mesh=mesh,
        in_specs=placed,
        out_specs=P(("groups", "ffn"), "hid"),
        check_vma=False,
    )
```

```python
import functools
import math

import jax
import jax.numpy as jnp
from jax import lax
from jax.experimental import pallas as pl
from jax.experimental.pallas import tpu as pltpu
from jax.sharding import PartitionSpec as P

HD = 128
NH = 8
MESH = pl.DeviceIdType.MESH
F32 = jnp.float32
BF16 = jnp.bfloat16


def kernel(
    nb,
    len_ref, slot_ref, x_hbm, wq_hbm, wk_hbm, wv_hbm, wo_hbm, kc_hbm, vc_hbm,
    out_ref,
    x, wq, wkv, wo, kc, vc,
    fkv, fq, skv, sq, rkv, rq,
    cos_s, sin_s, qf, kvf, sc, of, ag, lf, lhs, acc, fin,
    local_sem, rs_send, rs_recv, ag_send, ag_recv, fin_send, fin_recv,
):
    hid = 1 << nb
    h = lax.axis_index("hid")
    f = lax.axis_index("ffn")
    my = [lax.rem(lax.div(h, 1 << b), 2) for b in range(nb)]
    partner = [h + (1 - 2 * my[b]) * (1 << b) for b in range(nb)]
    rows = x.shape[0]
    rb = rows // hid
    nq = wq.shape[0]
    qw = wq.shape[2]
    orders = [tuple(range(nb)), (1, 0) + tuple(range(2, nb)) if nb > 1 else (0,)]

    def order_of(c):
        return orders[(c + 1) % 2]

    cp_x = pltpu.make_async_copy(x_hbm, x, local_sem.at[0])
    cp_k = pltpu.make_async_copy(wk_hbm, wkv.at[0], local_sem.at[1])
    cp_v = pltpu.make_async_copy(wv_hbm, wkv.at[1], local_sem.at[2])
    cp_kc = pltpu.make_async_copy(kc_hbm, kc, local_sem.at[3])
    cp_vc = pltpu.make_async_copy(vc_hbm, vc, local_sem.at[4])
    cp_q = [
        pltpu.make_async_copy(wq_hbm.at[:, pl.ds(c * qw, qw)], wq.at[c], local_sem.at[5 + c])
        for c in range(nq)
    ]
    cp_o = [
        pltpu.make_async_copy(
            wo_hbm.at[pl.ds(c * qw, qw), :], wo.at[c], local_sem.at[5 + nq + c]
        )
        for c in range(nq)
    ]
    cp_x.start()
    cp_k.start()
    cp_v.start()
    cp_q[0].start()
    cp_q[1].start()

    barrier = pltpu.get_barrier_semaphore()
    for b in range(nb):
        pl.semaphore_signal(barrier, inc=1, device_id={"hid": partner[b]}, device_id_type=MESH)
    pl.semaphore_signal(barrier, inc=1, device_id={"ffn": 1 - f}, device_id_type=MESH)

    lane = lax.broadcasted_iota(jnp.int32, (1, HD), 1)
    idx = jnp.where(lane < HD // 2, lane, lane - HD // 2).astype(F32)
    freq = jnp.exp(idx * (-2.0 * math.log(500000.0) / HD))
    for r in range(rb):
        cos_s[r : r + 1, :] = len_ref[r].astype(F32) * freq
    angle = cos_s[...]
    sign = jnp.where(lane < HD // 2, -1.0, 1.0).astype(F32)
    sin_s[...] = jnp.sin(angle) * sign
    cos_s[...] = jnp.cos(angle)

    def bufs(c):
        if c == 0:
            return fkv, skv, rkv, rb * 4
        return fq.at[c - 1], sq.at[c - 1], rq.at[c - 1], rb * NH

    def rs_copy(c, k):
        order = order_of(c)
        _, s, r, block = bufs(c)
        count = hid >> (k + 1)
        start = hid - (hid >> k)
        part = pl.ds(start * block, count * block)
        return pltpu.make_async_remote_copy(
            src_ref=s.at[part], dst_ref=r.at[part],
            send_sem=rs_send.at[c * nb + k], recv_sem=rs_recv.at[c * nb + k],
            device_id={"hid": partner[order[k]]}, device_id_type=MESH,
        )

    def rs_stage(c, k):
        order = order_of(c)
        sums, s, r, block = bufs(c)
        if k > 0:
            rs_copy(c, k - 1).wait_recv()
        left = nb - k - 1
        start = hid - (hid >> k)
        before = hid - (hid >> (k - 1)) if k > 0 else 0
        base = 0
        for j in range(k):
            base = base + my[order[j]] * (1 << order[j])

        def at(i, bit):
            off = 0
            for m in range(left):
                off += ((i >> (left - 1 - m)) & 1) << order[k + 1 + m]
            t = base + bit * (1 << order[k]) + off
            return pl.ds(pl.multiple_of(t * block, block), block)

        def came(i, bit):
            p = before + bit * (1 << left) + i
            return pl.ds(pl.multiple_of(p * block, block), block)

        mine = my[order[k]]
        for i in range(1 << left):
            value = sums[at(i, 1 - mine), :]
            if k > 0:
                value = value + r[came(i, 1 - mine), :].astype(F32)
            s[pl.ds((start + i) * block, block), :] = value.astype(BF16)
        rs_copy(c, k).start()
        if k > 0:
            for i in range(1 << left):
                sums[at(i, mine), :] = sums[at(i, mine), :] + r[came(i, mine), :].astype(F32)

    def rs_final(c):
        sums, s, r, block = bufs(c)
        rs_copy(c, nb - 1).wait_recv()
        own = pl.ds(pl.multiple_of(h * block, block), block)
        value = sums[own, :] + r[pl.ds((hid - 2) * block, block), :].astype(F32)
        if c == 0:
            kvf[...] = value
            return
        value = value.reshape(rb, NH, HD)
        turned = pltpu.roll(value.reshape(rb * NH, HD), HD // 2, 1).reshape(rb, NH, HD)
        cosine = cos_s[...][:, None, :]
        sine = sin_s[...][:, None, :]
        qf[:, (c - 1) * NH : c * NH, :] = value * cosine + turned * sine

    cp_x.wait()
    for part, cp in ((0, cp_k), (1, cp_v)):
        cp.wait()
        got = jnp.dot(x[...], wkv[part], preferred_element_type=F32)
        for j in range(2):
            fkv[pl.ds(part * 2 + j, rows, stride=4), :] = got[:, j * HD : (j + 1) * HD]
    pl.semaphore_wait(barrier, nb + 1)
    rs_stage(0, 0)

    for c in range(nq):
        cp_q[c].wait()
        if c + 2 < nq:
            cp_q[c + 2].start()
        elif c + 2 == nq:
            cp_kc.start()
            cp_vc.start()
            cp_o[0].start()
        else:
            for o in range(1, nq):
                cp_o[o].start()

        @pl.loop(0, qw // 256)
        def _(n):
            cols = pl.ds(pl.multiple_of(n * 256, 256), 256)
            got = jnp.dot(x[...], wq.at[c][:, cols], preferred_element_type=F32)
            for j in range(2):
                fq.at[c][pl.ds(n * 2 + j, rows, stride=NH), :] = got[:, j * HD : (j + 1) * HD]

        rs_stage(c + 1, 0)
        if nb > 1 and c >= 2:
            rs_stage(c - 2, 1)

    for k in range(1, nb + 1):
        for c in range(nq + 1):
            if k == nb:
                rs_final(c)
            elif k > 1 or c > nq - 3:
                rs_stage(c, k)

    heads = nq * NH
    slots = slot_ref.shape[1]
    spread = (
        lax.broadcasted_iota(jnp.int32, (slots, 2 * slots), 0)
        == lax.div(lax.broadcasted_iota(jnp.int32, (slots, 2 * slots), 1), 2)
    )
    spread = jnp.where(spread, 1.0, 0.0).astype(BF16)
    position = jnp.dot(
        slot_ref[...].astype(F32).astype(BF16), spread, preferred_element_type=F32
    )
    parity = (
        lax.rem(lax.broadcasted_iota(jnp.int32, (heads, 2 * slots), 1), 2)
        == lax.div(lax.broadcasted_iota(jnp.int32, (heads, 2 * slots), 0), heads // 2)
    )
    scale = 1.0 / math.sqrt(HD)
    cp_kc.wait()
    cp_vc.wait()
    for r in range(rb):
        sc[r] = lax.dot_general(
            qf[r].astype(BF16), kc[r], (((1,), (1,)), ((), ())), preferred_element_type=F32
        )
    kvrot = kvf[...]
    turned = pltpu.roll(kvrot, HD // 2, 1)
    for r in range(rb):
        def both(first, second):
            return jnp.concatenate(
                [
                    jnp.broadcast_to(first, (heads // 2, HD)),
                    jnp.broadcast_to(second, (heads // 2, HD)),
                ],
                axis=0,
            )

        cosine = cos_s[r : r + 1, :]
        sine = sin_s[r : r + 1, :]
        key = [
            (kvrot[r * 4 + g : r * 4 + g + 1] * cosine + turned[r * 4 + g : r * 4 + g + 1] * sine)
            for g in range(2)
        ]
        key = both(*key).astype(BF16).astype(F32)
        value = both(kvrot[r * 4 + 2 : r * 4 + 3], kvrot[r * 4 + 3 : r * 4 + 4])
        value = value.astype(BF16).astype(F32)
        query = qf[r].astype(BF16).astype(F32)
        own = jnp.sum(query * key, axis=-1, keepdims=True) * scale
        live = position[r : r + 1, :] < len_ref[r].astype(F32)
        scores = jnp.where(live & parity, sc[r] * scale, -jnp.inf)
        top = jnp.maximum(jnp.max(scores, axis=-1, keepdims=True), own)
        expo = jnp.exp(scores - top)
        own_expo = jnp.exp(own - top)
        over = 1.0 / (jnp.sum(expo, axis=-1, keepdims=True) + own_expo)
        weights = (expo * over).astype(BF16)
        own_weight = (own_expo * over).astype(BF16).astype(F32)
        got = jnp.dot(weights, vc[r], preferred_element_type=F32) + own_weight * value
        for c in range(nq):
            of[c, r * NH : (r + 1) * NH, :] = got[c * NH : (c + 1) * NH]

    block = rb * NH

    def place_of(c):
        place = 0
        for k in range(nb):
            place = place * 2 + my[order_of(c + 1)[k]]
        return place

    def ag_copy(c, k):
        start = lax.div(place_of(c), 1 << k) * (1 << k)
        part = pl.ds(pl.multiple_of(start * block, block), (1 << k) * block)
        return pltpu.make_async_remote_copy(
            src_ref=ag.at[c, part], dst_ref=ag.at[c, part],
            send_sem=ag_send.at[c * nb + k], recv_sem=ag_recv.at[c * nb + k],
            device_id={"hid": partner[order_of(c + 1)[nb - 1 - k]]}, device_id_type=MESH,
        )

    def position_of(c, t):
        p = 0
        for k in range(nb):
            p = p * 2 + ((t >> order_of(c + 1)[k]) & 1)
        return p

    half = rows // 2
    cols_out = out_ref.shape[1]
    tile = 512 if cols_out % 512 == 0 else cols_out
    tiles = cols_out // tile

    def fin_copy(n):
        cols = pl.ds(n * tile, tile)
        return pltpu.make_async_remote_copy(
            src_ref=acc.at[pl.ds(pl.multiple_of((1 - f) * half, half), half), cols],
            dst_ref=fin.at[:, cols],
            send_sem=fin_send.at[n], recv_sem=fin_recv.at[n],
            device_id={"ffn": 1 - f}, device_id_type=MESH,
        )

    def project(c):
        for t in range(hid):
            lf[t * block : (t + 1) * block, :] = ag[
                c, position_of(c, t) * block : (position_of(c, t) + 1) * block, :
            ].astype(F32)
        for j in range(NH):
            lhs[:, j * HD : (j + 1) * HD] = lf[pl.ds(j, rows, stride=NH), :].astype(BF16)
        cp_o[c].wait()
        for n in range(tiles):
            cols = pl.ds(n * tile, tile)
            got = jnp.dot(lhs[...], wo.at[c][:, cols], preferred_element_type=F32)
            if c == 0:
                acc[:, cols] = got
            else:
                acc[:, cols] = acc[:, cols] + got
            if c == nq - 1:
                fin_copy(n).start()

    for c in range(nq):
        own = pl.ds(pl.multiple_of(place_of(c) * block, block), block)
        ag[c, own, :] = of[c].astype(BF16)
        ag_copy(c, 0).start()
    for k in range(1, nb):
        for c in range(nq):
            ag_copy(c, k - 1).wait_recv()
            ag_copy(c, k).start()
    for c in range(nq):
        ag_copy(c, nb - 1).wait_recv()
        project(c)

    kept = pl.ds(pl.multiple_of(f * half, half), half)
    for n in range(tiles):
        cols = pl.ds(n * tile, tile)
        fin_copy(n).wait_recv()
        out_ref[:, cols] = (acc[kept, cols] + fin[:, cols]).astype(BF16)

    for c in range(nq + 1):
        for k in range(nb):
            rs_copy(c, k).wait_send()
    for c in range(nq):
        for k in range(nb):
            ag_copy(c, k).wait_send()
    for n in range(tiles):
        fin_copy(n).wait_send()


def per_device(hid, x, w_query, w_key, w_value, w_out, key_cache, value_cache, lengths, slot_pos):
    nb = hid.bit_length() - 1
    rows, depth = x.shape
    rb, slots, kvh, _ = key_cache.shape
    qcols = w_query.shape[1]
    qw = NH * HD
    nq = qcols // qw
    ncols = w_out.shape[1]
    tiles = ncols // 512 if ncols % 512 == 0 else 1
    kc = key_cache.reshape(rb, slots * kvh, HD)
    vc = value_cache.reshape(rb, slots * kvh, HD)
    anywhere = pl.BlockSpec(memory_space=pl.ANY)
    vmem = pltpu.VMEM
    return pl.pallas_call(
        functools.partial(kernel, nb),
        out_shape=jax.ShapeDtypeStruct((rows // 2, ncols), BF16),
        in_specs=[
            pl.BlockSpec(memory_space=pltpu.SMEM),
            pl.BlockSpec(memory_space=pltpu.VMEM),
        ] + [anywhere] * 7,
        out_specs=pl.BlockSpec(memory_space=pltpu.VMEM),
        scratch_shapes=[
            vmem((rows, depth), BF16),
            vmem((nq, depth, qw), BF16),
            vmem((2, depth, 2 * HD), BF16),
            vmem((nq, qw, ncols), BF16),
            vmem((rb, slots * kvh, HD), BF16),
            vmem((rb, slots * kvh, HD), BF16),
            vmem((rows * 4, HD), F32),
            vmem((nq, rows * NH, HD), F32),
            vmem(((hid - 1) * rb * 4, HD), BF16),
            vmem((nq, (hid - 1) * rb * NH, HD), BF16),
            vmem(((hid - 1) * rb * 4, HD), BF16),
            vmem((nq, (hid - 1) * rb * NH, HD), BF16),
            vmem((rb, HD), F32),
            vmem((rb, HD), F32),
            vmem((rb, nq * NH, HD), F32),
            vmem((rb * 4, HD), F32),
            vmem((rb, nq * NH, slots * kvh), F32),
            vmem((nq, rb * NH, HD), F32),
            vmem((nq, rows * NH, HD), BF16),
            vmem((rows * NH, HD), F32),
            vmem((rows, qw), BF16),
            vmem((rows, ncols), F32),
            vmem((rows // 2, ncols), F32),
            pltpu.SemaphoreType.DMA((5 + 2 * nq,)),
            pltpu.SemaphoreType.DMA(((nq + 1) * nb,)),
            pltpu.SemaphoreType.DMA(((nq + 1) * nb,)),
            pltpu.SemaphoreType.DMA((nq * nb,)),
            pltpu.SemaphoreType.DMA((nq * nb,)),
            pltpu.SemaphoreType.DMA((tiles,)),
            pltpu.SemaphoreType.DMA((tiles,)),
        ],
        compiler_params=pltpu.CompilerParams(
            collective_id=0, has_side_effects=True, vmem_limit_bytes=56 * 1024 * 1024
        ),
    )(lengths, slot_pos, x, w_query, w_key, w_value, w_out, kc, vc)


def solution(mesh):
    placed = (
        P("groups", "hid"),
        P("hid", "ffn"),
        P("hid", "ffn"),
        P("hid", "ffn"),
        P("ffn", "hid"),
        P(("groups", "hid"), None, "ffn", None),
        P(("groups", "hid"), None, "ffn", None),
        P(("groups", "hid")),
        P(("groups", "hid"), None),
    )
    return jax.shard_map(
        functools.partial(per_device, mesh.shape["hid"]),
        mesh=mesh,
        in_specs=placed,
        out_specs=P(("groups", "ffn"), "hid"),
        check_vma=False,
    )
```
